32 devices in a mesh: shot: 8 (over z, y), sub: 4 (over x, core).
Axes of the slice: x: 2, y: 2, z: 4, core: 2. Of those that a mesh axis runs over, the one named last changes fastest.
Arguments:
- background: float32 [3, 64, 192, 128], P(None, 'shot', 'sub'), may hold values from 0.55 to 2.4, as said below
- lanczos: float32 [3, 64, 192, 128], P(None, 'shot', 'sub'), may hold values from -6 to 6
- incident: float32 [8, 9, 16, 192, 128], P('shot', None, 'sub'), may hold values from -6 to 6
- receivers: int32 [8, 4, 256], P('shot', 'sub'), may hold values from 0 to 98303
- anchors: int32 [8], P('shot'), may hold values from 0 to 6, as said below
Outputs:
- hessian_vector: float32 [3, 64, 192, 128], P(None, 'shot', 'sub')
The draws below stay inside these ranges and needn't reach their ends.
Inputs may be any that keep to these rules, and one draw needn't show every extreme that they name: The footprint of shot s starts at model tile anchors[s], with s - 2 <= anchors[s] <= s; the last shot's footprint starts at tile 8 - 2. Channel 0 of background (first Lame parameter) lies within 1.2 to 2.4, channel 1 (shear modulus) within 0.6 to 1.2, channel 2 (buoyancy) within 0.55 to 1.1.
All inputs are finite; a program needn't handle non-finite values.
Results may differ from the reference program's by a relative error of at most 0.0003.
Values sent between devices are 32-bit elements; how exact they have to be, the bound alone decides.
A program may use at most 128 MiB of HBM per device.

```python
import jax
import jax.numpy as jnp
from jax import lax

SX = 4
FY = 192
FZ = 128
REC = 256
STEPS = 4
SHOTS = 8
SLABS = 4
TX = 8
FX = 16
MX = 64


def draw_anchors(key, part):
    key = jax.random.fold_in(key, 11)
    jitter = jax.random.randint(key, (SHOTS,), 0, 3)
    places = jnp.arange(SHOTS, dtype=jnp.int32) - 2 + jitter
    places = jnp.clip(places, 0, SHOTS - 2)
    return places.at[SHOTS - 1].set(SHOTS - 2).astype(jnp.int32)


def draw_background(key, part):
    key = jax.random.fold_in(key, 13)
    bottoms = jnp.array([1.2, 0.6, 0.55], jnp.float32).reshape(3, 1, 1, 1)
    ceilings = jnp.array([2.4, 1.2, 1.1], jnp.float32).reshape(3, 1, 1, 1)
    fraction = jax.random.uniform(key, (3, MX, FY, FZ), jnp.float32)
    fraction = fraction * fraction
    return ceilings - (ceilings - bottoms) * fraction


def plant(values, key, least, top_value):
    dims = values.shape
    place = [jax.random.randint(jax.random.fold_in(key, axis), (), 0, dims[axis]) for axis in range(len(dims))]
    values = values.at[tuple(place)].set(least)
    longest = dims.index(max(dims))
    place[longest] = (place[longest] + 1) % dims[longest]
    return values.at[tuple(place)].set(top_value)


def block_scale(own_key, dims, cuts, low, largest):
    def one(dim, blocks):
        draws = jax.random.uniform(jax.random.fold_in(jax.random.fold_in(own_key, 6), dim), (blocks,), jnp.float32, low / len(cuts), largest / len(cuts))
        return jnp.repeat(jnp.exp(draws), dims[dim] // blocks).reshape((-1,) + (1,) * (len(dims) - dim - 1))

    level = one(*cuts[0])
    for cut in cuts[1:]:
        level = level * one(*cut)
    return level


def noise(own_key, extent, width, limit, shards=(), kind=jnp.bfloat16):
    gain = block_scale(own_key, extent, shards, -0.22, 0.18) if shards else 1.0
    result = jax.random.normal(own_key, extent, jnp.float32) * width * gain
    return jnp.minimum(jnp.maximum(result, -limit), limit).astype(kind)


def setup_inputs(seed: int = 0) -> dict:
    arg_keys = jax.random.split(jax.random.key(seed), 6)
    background = draw_background(jax.random.fold_in(arg_keys[5], 71), 0)
    lanczos = noise(arg_keys[1], (3, MX, FY, FZ), 1.0, 6.0, ((1, 8), (2, 4)), jnp.float32)
    incident = noise(arg_keys[2], (SHOTS, 9, FX, FY, FZ), 1.0, 6.0, ((0, 8), (2, 4)), jnp.float32)
    receivers = plant(jax.random.randint(arg_keys[3], (SHOTS, SLABS, REC), 0, SX * FY * FZ), jax.random.fold_in(arg_keys[3], 1), 0, (SX * FY * FZ) - 1).astype(jnp.int32)
    anchors = draw_anchors(jax.random.fold_in(arg_keys[5], 71), 0)
    return dict(background=background, lanczos=lanczos, incident=incident, receivers=receivers, anchors=anchors)


time_step = 0.25


def lower_join(field, dimension, edge_rows):
    count = field.shape[dimension]
    return jnp.concatenate([edge_rows, lax.slice_in_dim(field, 0, count - 1, axis=dimension)], dimension)


def upper_join(field, dimension, edge_rows):
    count = field.shape[dimension]
    return jnp.concatenate([lax.slice_in_dim(field, 1, count, axis=dimension), edge_rows], dimension)


def zero_rows(field, dimension):
    return jnp.zeros_like(lax.slice_in_dim(field, 0, 1, axis=dimension))


def lower_diff(field, dimension, edge_rows):
    return field - lower_join(field, dimension, edge_rows)


def upper_diff(field, dimension, edge_rows):
    return upper_join(field, dimension, edge_rows) - field


def lower_local(field, dimension):
    return lower_diff(field, dimension, zero_rows(field, dimension))


def upper_local(field, dimension):
    return upper_diff(field, dimension, zero_rows(field, dimension))


def accelerate(stress, edge_rows):
    accel_x = lower_diff(stress[0], 0, edge_rows[0]) + lower_local(stress[3], 1) + lower_local(stress[4], 2)
    accel_y = lower_diff(stress[3], 0, edge_rows[1]) + lower_local(stress[1], 1) + lower_local(stress[5], 2)
    accel_z = lower_diff(stress[4], 0, edge_rows[2]) + lower_local(stress[5], 1) + lower_local(stress[2], 2)
    return jnp.stack([accel_x, accel_y, accel_z])


def strain(velocity, edge_rows):
    grad_xx = upper_diff(velocity[0], 0, edge_rows[0])
    grad_xy = upper_diff(velocity[1], 0, edge_rows[1])
    grad_xz = upper_diff(velocity[2], 0, edge_rows[2])
    normal_part = jnp.stack([grad_xx, upper_local(velocity[1], 1), upper_local(velocity[2], 2)])
    shear_part = jnp.stack([upper_local(velocity[0], 1) + grad_xy,
                            upper_local(velocity[0], 2) + grad_xz,
                            upper_local(velocity[1], 2) + upper_local(velocity[2], 1)])
    return normal_part, shear_part


def stress_rate(lame_first, shear, normal_part, shear_part):
    volume = normal_part[0] + normal_part[1] + normal_part[2]
    return volume, jnp.concatenate([lame_first * volume + 2.0 * shear * normal_part, shear * shear_part])


def stress_rims(stress):
    return jnp.stack([stress[0, -1:], stress[3, -1:], stress[4, -1:]])


def forward_pass(params, incoming, sensors, below_rims, above_rims):
    wave_vel = incoming[:3]
    wave_str = incoming[3:]
    born_vel = jnp.zeros_like(wave_vel)
    born_str = jnp.zeros_like(wave_str)
    records = []
    history = []
    for moment in range(STEPS):
        lower_rims = below_rims(jnp.stack([stress_rims(wave_str), stress_rims(born_str)]))
        wave_accel = accelerate(wave_str, lower_rims[0])
        born_accel = accelerate(born_str, lower_rims[1])
        wave_vel = wave_vel + time_step * params[2] * wave_accel
        born_vel = born_vel + time_step * (params[2] * born_accel + params[5] * wave_accel)
        upper_rims = above_rims(jnp.stack([wave_vel[:, :1], born_vel[:, :1]]))
        wave_normal, wave_shear = strain(wave_vel, upper_rims[0])
        born_normal, born_shear = strain(born_vel, upper_rims[1])
        wave_volume, wave_rate = stress_rate(params[0], params[1], wave_normal, wave_shear)
        born_rate = stress_rate(params[0], params[1], born_normal, born_shear)[1]
        scatter_rate = stress_rate(params[3], params[4], wave_normal, wave_shear)[1]
        wave_str = wave_str + time_step * wave_rate
        born_str = born_str + time_step * (born_rate + scatter_rate)
        records.append(born_vel[2].reshape(-1)[sensors])
        history.append((wave_accel, wave_volume, wave_normal, wave_shear))
    return records, history


def adjoint_pass(params, sensors, records, history, below_rims, above_rims, grid_shape):
    adj_vel = jnp.zeros((3,) + grid_shape, jnp.float32)
    adj_str = jnp.zeros((6,) + grid_shape, jnp.float32)
    image_lame = jnp.zeros(grid_shape, jnp.float32)
    image_shear = jnp.zeros(grid_shape, jnp.float32)
    image_buoy = jnp.zeros(grid_shape, jnp.float32)
    for moment in reversed(range(STEPS)):
        pushed = adj_vel[2].reshape(-1).at[sensors].add(records[moment]).reshape(grid_shape)
        adj_vel = jnp.stack([adj_vel[0], adj_vel[1], pushed])
        lower_rims = below_rims(stress_rims(adj_str)[None])
        adj_vel = adj_vel + time_step * params[2] * accelerate(adj_str, lower_rims[0])
        upper_rims = above_rims(adj_vel[:, :1][None])
        adj_normal, adj_shear = strain(adj_vel, upper_rims[0])
        adj_str = adj_str + time_step * stress_rate(params[0], params[1], adj_normal, adj_shear)[1]
        wave_accel, wave_volume, wave_normal, wave_shear = history[moment]
        image_lame = image_lame + wave_volume * (adj_str[0] + adj_str[1] + adj_str[2])
        image_shear = image_shear + 2.0 * (wave_normal[0] * adj_str[0] + wave_normal[1] * adj_str[1]
                                           + wave_normal[2] * adj_str[2]) + (
            wave_shear[0] * adj_str[3] + wave_shear[1] * adj_str[4] + wave_shear[2] * adj_str[5])
        image_buoy = image_buoy + (wave_accel[0] * adj_vel[0] + wave_accel[1] * adj_vel[1]
                                   + wave_accel[2] * adj_vel[2])
    return time_step * jnp.stack([image_lame, image_shear, image_buoy])


def no_rims(layers):
    return jnp.zeros_like(layers)


def reference(background, lanczos, incident, receivers, anchors):
    params_all = jnp.concatenate([background, lanczos], 0)
    slab_cells = SX * FY * FZ
    slab_starts = (jnp.arange(SLABS, dtype=jnp.int32) * slab_cells)[:, None]

    def one_shot(total, inputs):
        incoming, sensor_rows, anchor = inputs
        first_row = (anchor * TX).astype(jnp.int32)
        params = lax.dynamic_slice_in_dim(params_all, first_row, FX, 1)
        sensors = (sensor_rows.astype(jnp.int32) + slab_starts).reshape(-1)
        records, history = forward_pass(params, incoming, sensors, no_rims, no_rims)
        gradient = adjoint_pass(params, sensors, records, history, no_rims, no_rims, incoming.shape[1:])
        current = lax.dynamic_slice_in_dim(total, first_row, FX, 1)
        total = lax.dynamic_update_slice_in_dim(total, current + gradient, first_row, 1)
        return total, None

    total, unused = lax.scan(one_shot, jnp.zeros((3, MX, FY, FZ), jnp.float32), (incident, receivers, anchors))
    return total
```

```python
import functools

import jax
import jax.numpy as jnp
from jax import lax
from jax.experimental import pallas as pl
from jax.experimental.pallas import tpu as pltpu
from jax.sharding import PartitionSpec as P

STEPS = 4
BLOCK = 32
PAD = 8
time_step = 0.25
CHANNELS = (2, 5, 0, 1, 3, 4)
STRESS_FROM = (0, 3, 4, 1, 5, 2)


def kernel(
    shots, subs, back, lan, inc, gap, rec_row, rec_col, out,
    wv, ws, bv, bs, av, st, hist, rec, cnt, prm, img,
    gapp, ub, db, sb, yb, pp, gb, yout, yin, dout, din, uout, uin,
    load_sem, gap_sem, zup_sem, zdn_sem, y_sem, q_sem, loc_sem, rim_sem,
    gq_sem, gloc_sem, gy_sem, gd_sem, gu_sem,
):
    s = lax.axis_index("shot")
    me = lax.axis_index("sub")
    partner = s + 1 - 2 * (s % 2)
    even = s % 2 == 0
    odd = s % 2 == 1
    has_up = s + 2 < shots
    has_dn = s >= 2
    has_above = me + 1 < subs
    has_below = me >= 1
    rows_y = prm.shape[2]
    share = rows_y // subs
    slab = prm.shape[1]
    body = pl.ds(PAD, rows_y)

    def remote(src, dst, sems, index, device):
        return pltpu.make_async_remote_copy(
            src_ref=src, dst_ref=dst, send_sem=sems.at[(0,) + index], recv_sem=sems.at[(1,) + index],
            device_id=device, device_id_type=pl.DeviceIdType.MESH,
        )

    loads = [pltpu.make_async_copy(inc.at[f], wv.at[f, pl.ds(0, slab), body], load_sem.at[f]) for f in range(3)]
    loads += [
        pltpu.make_async_copy(inc.at[3 + STRESS_FROM[f]], ws.at[f, pl.ds(1, slab), body], load_sem.at[3 + f])
        for f in range(6)
    ]
    for load in loads:
        load.start()

    barrier = pltpu.get_barrier_semaphore()
    for k in range(1, subs):
        pl.semaphore_signal(barrier, inc=1, device_id={"sub": lax.rem(me + k, subs)}, device_id_type=pl.DeviceIdType.MESH)
    pl.semaphore_signal(barrier, inc=1, device_id={"shot": partner}, device_id_type=pl.DeviceIdType.MESH)

    @pl.when(has_up)
    def _():
        pl.semaphore_signal(barrier, inc=1, device_id={"shot": s + 2}, device_id_type=pl.DeviceIdType.MESH)

    @pl.when(has_dn)
    def _():
        pl.semaphore_signal(barrier, inc=1, device_id={"shot": s - 2}, device_id_type=pl.DeviceIdType.MESH)

    pl.semaphore_wait(barrier, subs + has_up.astype(jnp.int32) + has_dn.astype(jnp.int32))

    def tile(c):
        return back.at[c] if c < 3 else lan.at[c - 3]

    gap_copy = remote(gap, gapp, gap_sem, (), {"shot": partner})
    gap_copy.start()
    up_copy = lambda c: remote(tile(c), ub.at[c], zup_sem, (c,), {"shot": s + 2})
    dn_copy = lambda c: remote(tile(c), db.at[c], zdn_sem, (c,), {"shot": s - 2})
    y_copy = lambda c: remote(sb.at[c], yb.at[c], y_sem, (c,), {"shot": partner})

    @pl.when(has_up)
    def _():
        for c in CHANNELS:
            up_copy(c).start()

    @pl.when(jnp.logical_and(even, has_dn))
    def _():
        for c in CHANNELS:
            dn_copy(c).start()

    def zero_plane(ref):
        count, layers = ref.shape[0], ref.shape[1]

        def one(i, carry):
            ref[i // layers, i % layers] = jnp.zeros(ref.shape[2:], jnp.float32)
            return carry

        lax.fori_loop(0, count * layers, one, 0)

    for ref in (bv, bs, av, st, img):
        zero_plane(ref)

    def zero_rim(ref, layer):
        count, layers = ref.shape[0], ref.shape[1]

        def one(i, carry):
            zeros = jnp.zeros((PAD, ref.shape[3]), jnp.float32)
            ref[i // layers, i % layers, 0:PAD] = zeros
            ref[i // layers, i % layers, PAD + rows_y : 2 * PAD + rows_y] = zeros
            return carry

        lax.fori_loop(0, count * layers, one, 0)

    zero_rim(wv, slab)
    zero_rim(ws, 0)

    @pl.when(jnp.logical_not(has_above))
    def _():
        for f in range(3):
            wv[f, slab] = jnp.zeros(wv.shape[2:], jnp.float32)

    @pl.when(jnp.logical_not(has_below))
    def _():
        for f in range(3):
            ws[f, 0] = jnp.zeros(ws.shape[2:], jnp.float32)

    depth = cnt.shape[2]
    receivers = rec_row.shape[1]
    lanes = (rec_col[...] % depth == lax.broadcasted_iota(jnp.int32, (receivers, depth), 1))
    lanes = lanes.astype(jnp.float32).astype(jnp.bfloat16)
    row_of = rec_row[...] // depth

    def count_rows(x, carry):
        rows = lax.broadcasted_iota(jnp.int32, (rows_y, receivers), 0) + x * rows_y
        hot = (rows == row_of).astype(jnp.float32).astype(jnp.bfloat16)
        cnt[x] = jnp.dot(hot, lanes, preferred_element_type=jnp.float32)
        return carry

    lax.fori_loop(0, slab, count_rows, 0)

    for load in loads:
        load.wait()

    ws_rim = lambda: remote(ws.at[pl.ds(0, 3), slab, body], ws.at[pl.ds(0, 3), 0, body], rim_sem, (0,), {"sub": me + 1})
    bs_rim = lambda: remote(bs.at[pl.ds(0, 3), slab, body], bs.at[pl.ds(0, 3), 0, body], rim_sem, (1,), {"sub": me + 1})
    wv_rim = lambda: remote(wv.at[:, 0, body], wv.at[:, slab, body], rim_sem, (2,), {"sub": me - 1})
    bv_rim = lambda: remote(bv.at[:, 0, body], bv.at[:, slab, body], rim_sem, (3,), {"sub": me - 1})
    av_rim = lambda: remote(av.at[:, 0, body], av.at[:, slab, body], rim_sem, (4,), {"sub": me - 1})
    st_rim = lambda: remote(st.at[pl.ds(0, 3), slab, body], st.at[pl.ds(0, 3), 0, body], rim_sem, (5,), {"sub": me + 1})

    def when(*conditions):
        return pl.when(functools.reduce(jnp.logical_and, conditions))

    @pl.when(has_above)
    def _():
        ws_rim().start()

    gap_copy.wait()

    def each_plane(fn):
        def one(i, carry):
            fn(i // slab, i % slab)
            return carry

        lax.fori_loop(0, 2 * slab, one, 0)

    for c in CHANNELS:
        own = tile(c)

        @pl.when(has_dn)
        def _():
            up_copy(c).wait_recv()

        @when(even, has_up)
        def _():
            dn_copy(c).wait_recv()

        @pl.when(even)
        def _():
            each_plane(lambda h, x: sb.__setitem__((c, h, x), jnp.where(gapp[...] == 0.0, db[c, h, x], own[h, x])))

        @pl.when(odd)
        def _():
            each_plane(lambda h, x: sb.__setitem__((c, h, x), jnp.where(gapp[...] == 0.0, own[h, x], ub[c, h, x])))

        y_copy(c).start()

    def q_copy(c, k):
        to = lax.rem(me + k, subs)
        return remote(pp.at[c, to], prm.at[c, :, pl.ds(pl.multiple_of(me * share, 8), share)], q_sem, (c, k), {"sub": to})

    def q_own(c):
        return pltpu.make_async_copy(pp.at[c, me], prm.at[c, :, pl.ds(pl.multiple_of(me * share, 8), share)], loc_sem.at[c])

    for c in CHANNELS:
        own = tile(c)
        y_copy(c).wait_recv()

        def pick(h, x):
            g = gap[...]
            t, y, u = own[h, x], yb[c, h, x], ub[c, h, x]
            pp[c, h, x] = time_step * jnp.where(g == -2.0, u, jnp.where(g == -1.0, y, t))
            pp[c, 2 + h, x] = time_step * jnp.where(g == -1.0, t, y)

        each_plane(pick)
        for k in range(1, subs):
            q_copy(c, k).start()
        q_own(c).start()

    for c in CHANNELS:
        for k in range(1, subs):
            q_copy(c, k).wait()
        q_own(c).wait()
        y_copy(c).wait_send()

        @pl.when(has_up)
        def _():
            up_copy(c).wait_send()

        @when(even, has_dn)
        def _():
            dn_copy(c).wait_send()

    blocks = rows_y // BLOCK
    lane = lax.broadcasted_iota(jnp.int32, (BLOCK, depth), 1)

    def z_lower(v):
        return v - jnp.where(lane == 0, 0.0, pltpu.roll(v, 1, 1))

    def z_upper(v):
        return jnp.where(lane == depth - 1, 0.0, pltpu.roll(v, depth - 1, 1)) - v

    def rows(first, last, fn):
        def one(i, carry):
            x = i // blocks
            fn(x, pl.multiple_of((i % blocks) * BLOCK, BLOCK))
            return carry

        lax.fori_loop(first * blocks, last * blocks, one, 0)

    def accelerate(ref, x, y0):
        at = lambda f, dx, dy: ref[f, x + dx, pl.ds(y0 + PAD + dy, BLOCK), :]
        xx, xy, xz, yy, yz, zz = [at(f, 1, 0) for f in range(6)]
        ax = (xx - at(0, 0, 0)) + (xy - at(1, 1, -1)) + z_lower(xz)
        ay = (xy - at(1, 0, 0)) + (yy - at(3, 1, -1)) + z_lower(yz)
        az = (xz - at(2, 0, 0)) + (yz - at(4, 1, -1)) + z_lower(zz)
        return ax, ay, az

    def strain(ref, x, y0):
        at = lambda f, dx, dy: ref[f, x + dx, pl.ds(y0 + PAD + dy, BLOCK), :]
        vx, vy, vz = [at(f, 0, 0) for f in range(3)]
        normal = (at(0, 1, 0) - vx, at(1, 0, 1) - vy, z_upper(vz))
        shear = (
            (at(0, 0, 1) - vx) + (at(1, 1, 0) - vy),
            z_upper(vx) + (at(2, 1, 0) - vz),
            z_upper(vy) + (at(2, 0, 1) - vz),
        )
        return normal, shear

    def rate(lame, mu, normal, shear):
        first = lame * (normal[0] + normal[1] + normal[2])
        twice = 2.0 * mu
        return (
            first + twice * normal[0], mu * shear[0], mu * shear[1],
            first + twice * normal[1], mu * shear[2], first + twice * normal[2],
        )

    def param(c, x, y0):
        return prm[c, x, pl.ds(y0, BLOCK), :]

    def wave_velocity(t):
        def fn(x, y0):
            accel = accelerate(ws, x, y0)
            buoy = param(2, x, y0)
            for f in range(3):
                hist[t, f, x, pl.ds(y0, BLOCK), :] = accel[f]
                wv[f, x, pl.ds(y0 + PAD, BLOCK), :] += buoy * accel[f]

        return fn

    def born_velocity(t):
        def fn(x, y0):
            accel = accelerate(bs, x, y0)
            buoy, delta = param(2, x, y0), param(5, x, y0)
            for f in range(3):
                new = bv[f, x, pl.ds(y0 + PAD, BLOCK), :] + (
                    buoy * accel[f] + delta * hist[t, f, x, pl.ds(y0, BLOCK), :]
                )
                bv[f, x, pl.ds(y0 + PAD, BLOCK), :] = new
            rec[t, x, pl.ds(y0, BLOCK), :] = cnt[x, pl.ds(y0, BLOCK), :] * new

        return fn

    def wave_stress(t):
        def fn(x, y0):
            normal, shear = strain(wv, x, y0)
            for f in range(3):
                hist[t, 3 + f, x, pl.ds(y0, BLOCK), :] = normal[f]
                hist[t, 6 + f, x, pl.ds(y0, BLOCK), :] = shear[f]
            change = rate(param(0, x, y0), param(1, x, y0), normal, shear)
            for f in range(6):
                ws[f, x + 1, pl.ds(y0 + PAD, BLOCK), :] += change[f]

        return fn

    def born_stress(t):
        def fn(x, y0):
            normal, shear = strain(bv, x, y0)
            change = rate(param(0, x, y0), param(1, x, y0), normal, shear)
            wave_normal = [hist[t, 3 + f, x, pl.ds(y0, BLOCK), :] for f in range(3)]
            wave_shear = [hist[t, 6 + f, x, pl.ds(y0, BLOCK), :] for f in range(3)]
            scatter = rate(param(3, x, y0), param(4, x, y0), wave_normal, wave_shear)
            for f in range(6):
                bs[f, x + 1, pl.ds(y0 + PAD, BLOCK), :] += change[f] + scatter[f]

        return fn

    def forward(t, carry):
        later, more = t > 0, t < STEPS - 1
        rows(1, slab, wave_velocity(t))

        @pl.when(has_below)
        def _():
            ws_rim().wait_recv()

        @when(has_below, later)
        def _():
            wv_rim().wait_send()

        rows(0, 1, wave_velocity(t))

        @pl.when(has_below)
        def _():
            wv_rim().start()

        rows(1, slab, born_velocity(t))

        @when(has_below, later)
        def _():
            bs_rim().wait_recv()
            bv_rim().wait_send()

        rows(0, 1, born_velocity(t))

        @when(has_below, more)
        def _():
            bv_rim().start()

        rows(0, slab - 1, wave_stress(t))

        @pl.when(has_above)
        def _():
            wv_rim().wait_recv()
            ws_rim().wait_send()

        rows(slab - 1, slab, wave_stress(t))

        @when(has_above, more)
        def _():
            ws_rim().start()

        @pl.when(more)
        def _():
            rows(0, slab - 1, born_stress(t))

            @pl.when(has_above)
            def _():
                bv_rim().wait_recv()

            @when(has_above, later)
            def _():
                bs_rim().wait_send()

            rows(slab - 1, slab, born_stress(t))

            @pl.when(has_above)
            def _():
                bs_rim().start()

        return carry

    lax.fori_loop(0, STEPS, forward, 0)

    @pl.when(has_below)
    def _():
        wv_rim().wait_send()

    @pl.when(has_above)
    def _():
        bs_rim().wait_send()

    def adjoint_velocity(t):
        def fn(x, y0):
            accel = accelerate(st, x, y0)
            buoy = param(2, x, y0)
            total = img[2, x, pl.ds(y0, BLOCK), :]
            for f in range(3):
                old = av[f, x, pl.ds(y0 + PAD, BLOCK), :]
                if f == 2:
                    old = old + rec[t, x, pl.ds(y0, BLOCK), :]
                new = old + buoy * accel[f]
                av[f, x, pl.ds(y0 + PAD, BLOCK), :] = new
                total = total + hist[t, f, x, pl.ds(y0, BLOCK), :] * new
            img[2, x, pl.ds(y0, BLOCK), :] = total

        return fn

    def adjoint_stress(t):
        def fn(x, y0):
            normal, shear = strain(av, x, y0)
            change = rate(param(0, x, y0), param(1, x, y0), normal, shear)
            new = []
            for f in range(6):
                new.append(st[f, x + 1, pl.ds(y0 + PAD, BLOCK), :] + change[f])
                st[f, x + 1, pl.ds(y0 + PAD, BLOCK), :] = new[f]
            n0, n1, n2, h0, h1, h2 = [hist[t, 3 + f, x, pl.ds(y0, BLOCK), :] for f in range(6)]
            img[0, x, pl.ds(y0, BLOCK), :] += (n0 + n1 + n2) * (new[0] + new[3] + new[5])
            img[1, x, pl.ds(y0, BLOCK), :] += 2.0 * (n0 * new[0] + n1 * new[3] + n2 * new[5]) + (
                h0 * new[1] + h1 * new[2] + h2 * new[4]
            )

        return fn

    def adjoint(k, carry):
        t = STEPS - 1 - k
        later, more = k > 0, k < STEPS - 1
        rows(1, slab, adjoint_velocity(t))

        @when(has_below, later)
        def _():
            st_rim().wait_recv()
            av_rim().wait_send()

        rows(0, 1, adjoint_velocity(t))

        @pl.when(has_below)
        def _():
            av_rim().start()

        rows(0, slab - 1, adjoint_stress(t))

        @pl.when(has_above)
        def _():
            av_rim().wait_recv()

        @when(has_above, later)
        def _():
            st_rim().wait_send()

        rows(slab - 1, slab, adjoint_stress(t))

        @when(has_above, more)
        def _():
            st_rim().start()

        return carry

    lax.fori_loop(0, STEPS, adjoint, 0)

    @pl.when(has_below)
    def _():
        av_rim().wait_send()

    def g_copy(c, k):
        to = lax.rem(me + k, subs)
        return remote(img.at[c, :, pl.ds(pl.multiple_of(to * share, 8), share)], gb.at[c, me], gq_sem, (c, k), {"sub": to})

    def g_own(c):
        return pltpu.make_async_copy(img.at[c, :, pl.ds(pl.multiple_of(me * share, 8), share)], gb.at[c, me], gloc_sem.at[c])

    gy_copy = lambda c: remote(yout.at[c], yin.at[c], gy_sem, (c,), {"shot": partner})
    gd_copy = lambda c: remote(dout.at[c], din.at[c], gd_sem, (c,), {"shot": s - 2})
    gu_copy = lambda c: remote(uout.at[c], uin.at[c], gu_sem, (c,), {"shot": s + 2})

    for c in (2, 0, 1):
        for k in range(1, subs):
            g_copy(c, k).start()
        g_own(c).start()

    for c in (2, 0, 1):
        for k in range(1, subs):
            g_copy(c, k).wait_recv()
        g_own(c).wait()

        def split(h, x):
            g = gap[...]
            near, far = gb[c, h, x] * time_step, gb[c, 2 + h, x] * time_step
            yout[c, h, x] = jnp.where(g == -1.0, near, far)
            out[c, h, x] = jnp.where(g == -1.0, far, jnp.where(g == 0.0, near, 0.0))
            dout[c, h, x] = jnp.where(g == -2.0, near, 0.0)

        each_plane(split)
        gy_copy(c).start()

    for c in (2, 0, 1):
        gy_copy(c).wait_recv()

        @pl.when(even)
        def _():
            def pass_on(h, x):
                here = gapp[...] <= -1.0
                y = yin[c, h, x]
                out[c, h, x] += jnp.where(here, y, 0.0)
                uout[c, h, x] = jnp.where(here, 0.0, y)

            each_plane(pass_on)

        @pl.when(odd)
        def _():
            def pass_on(h, x):
                here = gapp[...] == 0.0
                y = yin[c, h, x]
                out[c, h, x] += jnp.where(here, y, 0.0)
                dout[c, h, x] += jnp.where(here, 0.0, y)

            each_plane(pass_on)

        @pl.when(has_dn)
        def _():
            gd_copy(c).start()

        @when(even, has_up)
        def _():
            gu_copy(c).start()

    for c in (2, 0, 1):
        @pl.when(has_up)
        def _():
            gd_copy(c).wait_recv()
            each_plane(lambda h, x: out.__setitem__((c, h, x), out[c, h, x] + din[c, h, x]))

        @when(even, has_dn)
        def _():
            gu_copy(c).wait_recv()
            each_plane(lambda h, x: out.__setitem__((c, h, x), out[c, h, x] + uin[c, h, x]))

    for c in (2, 0, 1):
        for k in range(1, subs):
            g_copy(c, k).wait_send()
        gy_copy(c).wait_send()

        @pl.when(has_dn)
        def _():
            gd_copy(c).wait_send()

        @when(even, has_up)
        def _():
            gu_copy(c).wait_send()


def on_device(shots, subs, background, lanczos, incident, receivers, anchors):
    slab, rows_y, depth = incident.shape[2:]
    share = background.shape[2]
    halves = background.shape[1] // slab
    gap = anchors[0] - lax.axis_index("shot")
    gap = jnp.full((share, depth), gap.astype(jnp.float32))
    cut = lambda a: a.reshape(3, halves, slab, share, depth)
    f32 = jnp.float32
    tile = (halves, slab, share, depth)
    plane = (rows_y + 2 * PAD, depth)
    vel, stress = (3, slab + 1) + plane, (6, slab + 1) + plane
    vmem = lambda *shape: pltpu.VMEM(shape, f32)
    dma = lambda *shape: pltpu.SemaphoreType.DMA(shape)
    scratch = [
        vmem(*vel), vmem(*stress), vmem(*vel), vmem(*stress), vmem(*vel), vmem(*stress),
        vmem(STEPS, 9, slab, rows_y, depth), vmem(STEPS, slab, rows_y, depth), vmem(slab, rows_y, depth),
        vmem(6, slab, rows_y, depth), vmem(3, slab, rows_y, depth),
        vmem(share, depth), vmem(6, *tile), vmem(6, *tile), vmem(6, *tile), vmem(6, *tile),
        vmem(6, 2 * halves, slab, share, depth), vmem(3, 2 * halves, slab, share, depth),
        vmem(3, *tile), vmem(3, *tile), vmem(3, *tile), vmem(3, *tile), vmem(3, *tile), vmem(3, *tile),
        dma(9), dma(2), dma(2, 6), dma(2, 6), dma(2, 6), dma(2, 6, subs), dma(6), dma(2, 6),
        dma(2, 3, subs), dma(3), dma(2, 3), dma(2, 3), dma(2, 3),
    ]
    whole = pl.BlockSpec(memory_space=pltpu.VMEM)
    result = pl.pallas_call(
        functools.partial(kernel, shots, subs),
        out_shape=jax.ShapeDtypeStruct((3,) + tile, f32),
        in_specs=[whole, whole, pl.BlockSpec(memory_space=pl.ANY), whole, whole, whole],
        out_specs=whole,
        scratch_shapes=scratch,
        compiler_params=pltpu.CompilerParams(
            collective_id=0, has_side_effects=True, vmem_limit_bytes=60 * 1024 * 1024
        ),
    )(
        cut(background), cut(lanczos), incident[0], gap,
        receivers.reshape(1, -1), receivers.reshape(-1, 1),
    )
    return result.reshape(background.shape)


def solution(mesh):
    placed = (
        P(None, "shot", "sub", None),
        P(None, "shot", "sub", None),
        P("shot", None, "sub", None, None),
        P("shot", "sub", None),
        P("shot"),
    )
    return jax.shard_map(
        functools.partial(on_device, mesh.shape["shot"], mesh.shape["sub"]),
        mesh=mesh,
        in_specs=placed,
        out_specs=P(None, "shot", "sub", None),
        check_vma=False,
    )
```

```python
import functools

import jax
import jax.numpy as jnp
from jax import lax
from jax.experimental import pallas as pl
from jax.experimental.pallas import tpu as pltpu
from jax.sharding import PartitionSpec as P

STEPS = 4
BLOCK = 32
PAD = 8
time_step = 0.25
WINDOW = 2
CHANNELS = (2, 5, 0, 1, 3, 4)
STRESS_FROM = (0, 3, 4, 1, 5, 2)


def kernel(
    shots, subs, back, lan, inc, gap, rec_row, rec_col, out,
    wv, ws, bv, bs, av, st, hist, rec, cnt, prm, img,
    gapp, ub, db, sb, yb, pp, gb, yout, yin, dout, din, uout, uin,
    load_sem, gap_sem, zup_sem, zdn_sem, y_sem, q_sem, loc_sem, rim_sem,
    gq_sem, gloc_sem, gy_sem, gd_sem, gu_sem,
):
    s = lax.axis_index("shot")
    me = lax.axis_index("sub")
    partner = s + 1 - 2 * (s % 2)
    even = s % 2 == 0
    odd = s % 2 == 1
    has_up = s + 2 < shots
    has_dn = s >= 2
    has_above = me + 1 < subs
    has_below = me >= 1
    rows_y = prm.shape[2]
    share = rows_y // subs
    slab = prm.shape[1]
    body = pl.ds(PAD, rows_y)

    def remote(src, dst, sems, index, device):
        return pltpu.make_async_remote_copy(
            src_ref=src, dst_ref=dst, send_sem=sems.at[(0,) + index], recv_sem=sems.at[(1,) + index],
            device_id=device, device_id_type=pl.DeviceIdType.MESH,
        )

    loads = [pltpu.make_async_copy(inc.at[f], wv.at[f, pl.ds(0, slab), body], load_sem.at[f]) for f in range(3)]
    loads += [
        pltpu.make_async_copy(inc.at[3 + STRESS_FROM[f]], ws.at[f, pl.ds(1, slab), body], load_sem.at[3 + f])
        for f in range(6)
    ]
    for load in loads:
        load.start()

    barrier = pltpu.get_barrier_semaphore()
    for k in range(1, subs):
        pl.semaphore_signal(barrier, inc=1, device_id={"sub": lax.rem(me + k, subs)}, device_id_type=pl.DeviceIdType.MESH)
    pl.semaphore_signal(barrier, inc=1, device_id={"shot": partner}, device_id_type=pl.DeviceIdType.MESH)

    @pl.when(has_up)
    def _():
        pl.semaphore_signal(barrier, inc=1, device_id={"shot": s + 2}, device_id_type=pl.DeviceIdType.MESH)

    @pl.when(has_dn)
    def _():
        pl.semaphore_signal(barrier, inc=1, device_id={"shot": s - 2}, device_id_type=pl.DeviceIdType.MESH)

    pl.semaphore_wait(barrier, subs + has_up.astype(jnp.int32) + has_dn.astype(jnp.int32))

    def tile(c):
        return back.at[c] if c < 3 else lan.at[c - 3]

    gap_copy = remote(gap, gapp, gap_sem, (), {"shot": partner})
    gap_copy.start()
    up_copy = lambda c: remote(tile(c), ub.at[c], zup_sem, (c,), {"shot": s + 2})
    dn_copy = lambda c: remote(tile(c), db.at[c], zdn_sem, (c,), {"shot": s - 2})
    y_copy = lambda c: remote(sb.at[c], yb.at[c], y_sem, (c,), {"shot": partner})

    def send_tile(c):
        @pl.when(has_up)
        def _():
            up_copy(c).start()

        @pl.when(jnp.logical_and(even, has_dn))
        def _():
            dn_copy(c).start()

    for c in CHANNELS[:WINDOW]:
        send_tile(c)

    def zero_plane(ref):
        count, layers = ref.shape[0], ref.shape[1]

        def one(i, carry):
            ref[i // layers, i % layers] = jnp.zeros(ref.shape[2:], jnp.float32)
            return carry

        lax.fori_loop(0, count * layers, one, 0)

    for ref in (bv, bs, av, st, img):
        zero_plane(ref)

    def zero_rim(ref, layer):
        count, layers = ref.shape[0], ref.shape[1]

        def one(i, carry):
            zeros = jnp.zeros((PAD, ref.shape[3]), jnp.float32)
            ref[i // layers, i % layers, 0:PAD] = zeros
            ref[i // layers, i % layers, PAD + rows_y : 2 * PAD + rows_y] = zeros
            return carry

        lax.fori_loop(0, count * layers, one, 0)

    zero_rim(wv, slab)
    zero_rim(ws, 0)

    @pl.when(jnp.logical_not(has_above))
    def _():
        for f in range(3):
            wv[f, slab] = jnp.zeros(wv.shape[2:], jnp.float32)

    @pl.when(jnp.logical_not(has_below))
    def _():
        for f in range(3):
            ws[f, 0] = jnp.zeros(ws.shape[2:], jnp.float32)

    depth = cnt.shape[2]
    receivers = rec_row.shape[1]
    lanes = (rec_col[...] % depth == lax.broadcasted_iota(jnp.int32, (receivers, depth), 1))
    lanes = lanes.astype(jnp.float32).astype(jnp.bfloat16)
    row_of = rec_row[...] // depth

    def count_rows(x, carry):
        rows = lax.broadcasted_iota(jnp.int32, (rows_y, receivers), 0) + x * rows_y
        hot = (rows == row_of).astype(jnp.float32).astype(jnp.bfloat16)
        cnt[x] = jnp.dot(hot, lanes, preferred_element_type=jnp.float32)
        return carry

    lax.fori_loop(0, slab, count_rows, 0)

    for load in loads:
        load.wait()

    ws_rim = lambda: remote(ws.at[pl.ds(0, 3), slab, body], ws.at[pl.ds(0, 3), 0, body], rim_sem, (0,), {"sub": me + 1})
    bs_rim = lambda: remote(bs.at[pl.ds(0, 3), slab, body], bs.at[pl.ds(0, 3), 0, body], rim_sem, (1,), {"sub": me + 1})
    wv_rim = lambda: remote(wv.at[:, 0, body], wv.at[:, slab, body], rim_sem, (2,), {"sub": me - 1})
    bv_rim = lambda: remote(bv.at[:, 0, body], bv.at[:, slab, body], rim_sem, (3,), {"sub": me - 1})
    av_rim = lambda: remote(av.at[:, 0, body], av.at[:, slab, body], rim_sem, (4,), {"sub": me - 1})
    st_rim = lambda: remote(st.at[pl.ds(0, 3), slab, body], st.at[pl.ds(0, 3), 0, body], rim_sem, (5,), {"sub": me + 1})

    def when(*conditions):
        return pl.when(functools.reduce(jnp.logical_and, conditions))

    @pl.when(has_above)
    def _():
        ws_rim().start()

    gap_copy.wait()

    def each_plane(fn):
        def one(i, carry):
            fn(i // slab, i % slab)
            return carry

        lax.fori_loop(0, 2 * slab, one, 0)

    def hand_on(c):
        own = tile(c)

        @pl.when(has_dn)
        def _():
            up_copy(c).wait_recv()

        @when(even, has_up)
        def _():
            dn_copy(c).wait_recv()

        @pl.when(even)
        def _():
            each_plane(lambda h, x: sb.__setitem__((c, h, x), jnp.where(gapp[...] == 0.0, db[c, h, x], own[h, x])))

        @pl.when(odd)
        def _():
            each_plane(lambda h, x: sb.__setitem__((c, h, x), jnp.where(gapp[...] == 0.0, own[h, x], ub[c, h, x])))

        y_copy(c).start()

        @pl.when(has_up)
        def _():
            up_copy(c).wait_send()

        @when(even, has_dn)
        def _():
            dn_copy(c).wait_send()

    def q_copy(c, k):
        to = lax.rem(me + k, subs)
        return remote(pp.at[c, to], prm.at[c, :, pl.ds(pl.multiple_of(me * share, 8), share)], q_sem, (c, k), {"sub": to})

    def q_own(c):
        return pltpu.make_async_copy(pp.at[c, me], prm.at[c, :, pl.ds(pl.multiple_of(me * share, 8), share)], loc_sem.at[c])

    def share_out(c):
        own = tile(c)
        y_copy(c).wait_recv()

        def pick(h, x):
            g = gap[...]
            t, y, u = own[h, x], yb[c, h, x], ub[c, h, x]
            pp[c, h, x] = time_step * jnp.where(g == -2.0, u, jnp.where(g == -1.0, y, t))
            pp[c, 2 + h, x] = time_step * jnp.where(g == -1.0, t, y)

        each_plane(pick)
        for k in range(1, subs):
            q_copy(c, k).start()
        q_own(c).start()

    def shared(c):
        for k in range(1, subs):
            q_copy(c, k).wait_recv()
        q_own(c).wait()

    blocks = rows_y // BLOCK
    lane = lax.broadcasted_iota(jnp.int32, (BLOCK, depth), 1)

    def z_lower(v):
        return v - jnp.where(lane == 0, 0.0, pltpu.roll(v, 1, 1))

    def z_upper(v):
        return jnp.where(lane == depth - 1, 0.0, pltpu.roll(v, depth - 1, 1)) - v

    def rows(first, last, fn):
        def one(i, carry):
            x = i // blocks
            fn(x, pl.multiple_of((i % blocks) * BLOCK, BLOCK))
            return carry

        lax.fori_loop(first * blocks, last * blocks, one, 0)

    def accelerate(ref, x, y0):
        at = lambda f, dx, dy: ref[f, x + dx, pl.ds(y0 + PAD + dy, BLOCK), :]
        xx, xy, xz, yy, yz, zz = [at(f, 1, 0) for f in range(6)]
        ax = (xx - at(0, 0, 0)) + (xy - at(1, 1, -1)) + z_lower(xz)
        ay = (xy - at(1, 0, 0)) + (yy - at(3, 1, -1)) + z_lower(yz)
        az = (xz - at(2, 0, 0)) + (yz - at(4, 1, -1)) + z_lower(zz)
        return ax, ay, az

    def strain(ref, x, y0):
        at = lambda f, dx, dy: ref[f, x + dx, pl.ds(y0 + PAD + dy, BLOCK), :]
        vx, vy, vz = [at(f, 0, 0) for f in range(3)]
        normal = (at(0, 1, 0) - vx, at(1, 0, 1) - vy, z_upper(vz))
        shear = (
            (at(0, 0, 1) - vx) + (at(1, 1, 0) - vy),
            z_upper(vx) + (at(2, 1, 0) - vz),
            z_upper(vy) + (at(2, 0, 1) - vz),
        )
        return normal, shear

    def rate(lame, mu, normal, shear):
        first = lame * (normal[0] + normal[1] + normal[2])
        twice = 2.0 * mu
        return (
            first + twice * normal[0], mu * shear[0], mu * shear[1],
            first + twice * normal[1], mu * shear[2], first + twice * normal[2],
        )

    def param(c, x, y0):
        return prm[c, x, pl.ds(y0, BLOCK), :]

    def wave_velocity(t):
        def fn(x, y0):
            accel = accelerate(ws, x, y0)
            buoy = param(2, x, y0)
            for f in range(3):
                hist[t, f, x, pl.ds(y0, BLOCK), :] = accel[f]
                wv[f, x, pl.ds(y0 + PAD, BLOCK), :] += buoy * accel[f]

        return fn

    def born_velocity(t):
        def fn(x, y0):
            accel = accelerate(bs, x, y0)
            buoy, delta = param(2, x, y0), param(5, x, y0)
            for f in range(3):
                new = bv[f, x, pl.ds(y0 + PAD, BLOCK), :] + (
                    buoy * accel[f] + delta * hist[t, f, x, pl.ds(y0, BLOCK), :]
                )
                bv[f, x, pl.ds(y0 + PAD, BLOCK), :] = new
            rec[t, x, pl.ds(y0, BLOCK), :] = cnt[x, pl.ds(y0, BLOCK), :] * new

        return fn

    def born_first(x, y0):
        delta = param(5, x, y0)
        for f in range(3):
            new = delta * hist[0, f, x, pl.ds(y0, BLOCK), :]
            bv[f, x, pl.ds(y0 + PAD, BLOCK), :] = new
        rec[0, x, pl.ds(y0, BLOCK), :] = cnt[x, pl.ds(y0, BLOCK), :] * new

    def born_last(x, y0):
        t = STEPS - 1
        accel = accelerate(bs, x, y0)[2]
        new = bv[2, x, pl.ds(y0 + PAD, BLOCK), :] + (
            param(2, x, y0) * accel + param(5, x, y0) * hist[t, 2, x, pl.ds(y0, BLOCK), :]
        )
        rec[t, x, pl.ds(y0, BLOCK), :] = cnt[x, pl.ds(y0, BLOCK), :] * new

    def wave_stress(t):
        def fn(x, y0):
            normal, shear = strain(wv, x, y0)
            for f in range(3):
                hist[t, 3 + f, x, pl.ds(y0, BLOCK), :] = normal[f]
                hist[t, 6 + f, x, pl.ds(y0, BLOCK), :] = shear[f]
            if t == STEPS - 1:
                return
            change = rate(param(0, x, y0), param(1, x, y0), normal, shear)
            for f in range(6):
                ws[f, x + 1, pl.ds(y0 + PAD, BLOCK), :] += change[f]

        return fn

    def born_stress(t):
        def fn(x, y0):
            normal, shear = strain(bv, x, y0)
            change = rate(param(0, x, y0), param(1, x, y0), normal, shear)
            wave_normal = [hist[t, 3 + f, x, pl.ds(y0, BLOCK), :] for f in range(3)]
            wave_shear = [hist[t, 6 + f, x, pl.ds(y0, BLOCK), :] for f in range(3)]
            scatter = rate(param(3, x, y0), param(4, x, y0), wave_normal, wave_shear)
            for f in range(6):
                bs[f, x + 1, pl.ds(y0 + PAD, BLOCK), :] += change[f] + scatter[f]

        return fn

    def below(*copies):
        @pl.when(has_below)
        def _():
            for act in copies:
                act()

    def above(*copies):
        @pl.when(has_above)
        def _():
            for act in copies:
                act()

    def stresses(t):
        if t == 0:
            shared(0)
            shared(1)
        rows(0, slab - 1, wave_stress(t))
        above(lambda: wv_rim().wait_recv(), lambda: ws_rim().wait_send())
        rows(slab - 1, slab, wave_stress(t))
        if t == STEPS - 1:
            return
        above(lambda: ws_rim().start())
        if t == 0:
            shared(3)
            shared(4)
        rows(0, slab - 1, born_stress(t))
        above(lambda: bv_rim().wait_recv())
        if t > 0:
            above(lambda: bs_rim().wait_send())
        rows(slab - 1, slab, born_stress(t))
        above(lambda: bs_rim().start())

    count = len(CHANNELS)
    for i in range(count + 1):
        if i < count:
            hand_on(CHANNELS[i])
            if i + WINDOW < count:
                send_tile(CHANNELS[i + WINDOW])
        if i >= 1:
            share_out(CHANNELS[i - 1])
        if i == 3:
            shared(2)
            rows(1, slab, wave_velocity(0))
        if i == 4:
            below(lambda: ws_rim().wait_recv())
            rows(0, 1, wave_velocity(0))
            below(lambda: wv_rim().start())
        if i == 5:
            shared(5)
            rows(0, 1, born_first)
            below(lambda: bv_rim().start())
            rows(1, slab, born_first)
    stresses(0)

    for t in range(1, STEPS):
        last = t == STEPS - 1
        rows(1, slab, wave_velocity(t))
        below(lambda: ws_rim().wait_recv(), lambda: wv_rim().wait_send())
        rows(0, 1, wave_velocity(t))
        below(lambda: wv_rim().start())
        born = born_last if last else born_velocity(t)
        rows(1, slab, born)
        below(lambda: bs_rim().wait_recv(), lambda: bv_rim().wait_send())
        rows(0, 1, born)
        if not last:
            below(lambda: bv_rim().start())
        stresses(t)

    below(lambda: wv_rim().wait_send())
    above(lambda: bs_rim().wait_send())

    def adjoint_first(x, y0):
        new = rec[STEPS - 1, x, pl.ds(y0, BLOCK), :]
        av[2, x, pl.ds(y0 + PAD, BLOCK), :] = new
        img[2, x, pl.ds(y0, BLOCK), :] = hist[STEPS - 1, 2, x, pl.ds(y0, BLOCK), :] * new

    def adjoint_velocity(t):
        def fn(x, y0):
            accel = accelerate(st, x, y0)
            buoy = param(2, x, y0)
            total = img[2, x, pl.ds(y0, BLOCK), :]
            for f in range(3):
                old = av[f, x, pl.ds(y0 + PAD, BLOCK), :]
                if f == 2:
                    old = old + rec[t, x, pl.ds(y0, BLOCK), :]
                new = old + buoy * accel[f]
                av[f, x, pl.ds(y0 + PAD, BLOCK), :] = new
                total = total + hist[t, f, x, pl.ds(y0, BLOCK), :] * new
            img[2, x, pl.ds(y0, BLOCK), :] = total

        return fn

    def adjoint_stress(t):
        def fn(x, y0):
            normal, shear = strain(av, x, y0)
            change = rate(param(0, x, y0), param(1, x, y0), normal, shear)
            new = []
            for f in range(6):
                new.append(st[f, x + 1, pl.ds(y0 + PAD, BLOCK), :] + change[f])
                st[f, x + 1, pl.ds(y0 + PAD, BLOCK), :] = new[f]
            n0, n1, n2, h0, h1, h2 = [hist[t, 3 + f, x, pl.ds(y0, BLOCK), :] for f in range(6)]
            img[0, x, pl.ds(y0, BLOCK), :] += (n0 + n1 + n2) * (new[0] + new[3] + new[5])
            img[1, x, pl.ds(y0, BLOCK), :] += 2.0 * (n0 * new[0] + n1 * new[3] + n2 * new[5]) + (
                h0 * new[1] + h1 * new[2] + h2 * new[4]
            )

        return fn

    def g_copy(c, k):
        to = lax.rem(me + k, subs)
        return remote(img.at[c, :, pl.ds(pl.multiple_of(to * share, 8), share)], gb.at[c, me], gq_sem, (c, k), {"sub": to})

    def g_own(c):
        return pltpu.make_async_copy(img.at[c, :, pl.ds(pl.multiple_of(me * share, 8), share)], gb.at[c, me], gloc_sem.at[c])

    gy_copy = lambda c: remote(yout.at[c], yin.at[c], gy_sem, (c,), {"shot": partner})
    gd_copy = lambda c: remote(dout.at[c], din.at[c], gd_sem, (c,), {"shot": s - 2})
    gu_copy = lambda c: remote(uout.at[c], uin.at[c], gu_sem, (c,), {"shot": s + 2})

    def send_image(c):
        for k in range(1, subs):
            g_copy(c, k).start()
        g_own(c).start()

    first_rim = lambda: remote(
        av.at[pl.ds(2, 1), 0, body], av.at[pl.ds(2, 1), slab, body], rim_sem, (4,), {"sub": me - 1}
    )
    for k in range(STEPS):
        t = STEPS - 1 - k
        rim = av_rim if k else first_rim
        if k == 0:
            rows(0, slab, adjoint_first)
        else:
            rows(1, slab, adjoint_velocity(t))
            below(lambda: st_rim().wait_recv(), lambda: (av_rim if k > 1 else first_rim)().wait_send())
            rows(0, 1, adjoint_velocity(t))
        below(lambda: rim().start())
        rows(0, slab - 1, adjoint_stress(t))
        if k == STEPS - 1:
            send_image(2)
        above(lambda: rim().wait_recv())
        if k > 0:
            above(lambda: st_rim().wait_send())
        rows(slab - 1, slab, adjoint_stress(t))
        if k < STEPS - 1:
            above(lambda: st_rim().start())

    below(lambda: av_rim().wait_send())
    send_image(0)
    send_image(1)

    def to_partner(c):
        for k in range(1, subs):
            g_copy(c, k).wait_recv()
        g_own(c).wait()

        def split(h, x):
            g = gap[...]
            near, far = gb[c, h, x] * time_step, gb[c, 2 + h, x] * time_step
            yout[c, h, x] = jnp.where(g == -1.0, near, far)
            out[c, h, x] = jnp.where(g == -1.0, far, jnp.where(g == 0.0, near, 0.0))
            dout[c, h, x] = jnp.where(g == -2.0, near, 0.0)

        each_plane(split)
        gy_copy(c).start()

    def along(c):
        gy_copy(c).wait_recv()

        @pl.when(even)
        def _():
            def pass_on(h, x):
                here = gapp[...] <= -1.0
                y = yin[c, h, x]
                out[c, h, x] += jnp.where(here, y, 0.0)
                uout[c, h, x] = jnp.where(here, 0.0, y)

            each_plane(pass_on)

        @pl.when(odd)
        def _():
            def pass_on(h, x):
                here = gapp[...] == 0.0
                y = yin[c, h, x]
                out[c, h, x] += jnp.where(here, y, 0.0)
                dout[c, h, x] += jnp.where(here, 0.0, y)

            each_plane(pass_on)

        @pl.when(has_dn)
        def _():
            gd_copy(c).start()

        @when(even, has_up)
        def _():
            gu_copy(c).start()

    def collect(c):
        @pl.when(has_up)
        def _():
            gd_copy(c).wait_recv()
            each_plane(lambda h, x: out.__setitem__((c, h, x), out[c, h, x] + din[c, h, x]))

        @when(even, has_dn)
        def _():
            gu_copy(c).wait_recv()
            each_plane(lambda h, x: out.__setitem__((c, h, x), out[c, h, x] + uin[c, h, x]))

    images = (2, 0, 1)
    for i in range(len(images) + 2):
        if i < len(images):
            to_partner(images[i])
        if 1 <= i <= len(images):
            along(images[i - 1])
        if i >= 2:
            collect(images[i - 2])

    for c in CHANNELS:
        for k in range(1, subs):
            q_copy(c, k).wait_send()
        y_copy(c).wait_send()

    for c in (2, 0, 1):
        for k in range(1, subs):
            g_copy(c, k).wait_send()
        gy_copy(c).wait_send()

        @pl.when(has_dn)
        def _():
            gd_copy(c).wait_send()

        @when(even, has_up)
        def _():
            gu_copy(c).wait_send()


def on_device(shots, subs, background, lanczos, incident, receivers, anchors):
    slab, rows_y, depth = incident.shape[2:]
    share = background.shape[2]
    halves = background.shape[1] // slab
    gap = anchors[0] - lax.axis_index("shot")
    gap = jnp.full((share, depth), gap.astype(jnp.float32))
    cut = lambda a: a.reshape(3, halves, slab, share, depth)
    f32 = jnp.float32
    tile = (halves, slab, share, depth)
    plane = (rows_y + 2 * PAD, depth)
    vel, stress = (3, slab + 1) + plane, (6, slab + 1) + plane
    vmem = lambda *shape: pltpu.VMEM(shape, f32)
    dma = lambda *shape: pltpu.SemaphoreType.DMA(shape)
    scratch = [
        vmem(*vel), vmem(*stress), vmem(*vel), vmem(*stress), vmem(*vel), vmem(*stress),
        vmem(STEPS, 9, slab, rows_y, depth), vmem(STEPS, slab, rows_y, depth), vmem(slab, rows_y, depth),
        vmem(6, slab, rows_y, depth), vmem(3, slab, rows_y, depth),
        vmem(share, depth), vmem(6, *tile), vmem(6, *tile), vmem(6, *tile), vmem(6, *tile),
        vmem(6, 2 * halves, slab, share, depth), vmem(3, 2 * halves, slab, share, depth),
        vmem(3, *tile), vmem(3, *tile), vmem(3, *tile), vmem(3, *tile), vmem(3, *tile), vmem(3, *tile),
        dma(9), dma(2), dma(2, 6), dma(2, 6), dma(2, 6), dma(2, 6, subs), dma(6), dma(2, 6),
        dma(2, 3, subs), dma(3), dma(2, 3), dma(2, 3), dma(2, 3),
    ]
    whole = pl.BlockSpec(memory_space=pltpu.VMEM)
    result = pl.pallas_call(
        functools.partial(kernel, shots, subs),
        out_shape=jax.ShapeDtypeStruct((3,) + tile, f32),
        in_specs=[whole, whole, pl.BlockSpec(memory_space=pl.ANY), whole, whole, whole],
        out_specs=whole,
        scratch_shapes=scratch,
        compiler_params=pltpu.CompilerParams(
            collective_id=0, has_side_effects=True, vmem_limit_bytes=60 * 1024 * 1024
        ),
    )(
        cut(background), cut(lanczos), incident[0], gap,
        receivers.reshape(1, -1), receivers.reshape(-1, 1),
    )
    return result.reshape(background.shape)


def solution(mesh):
    placed = (
        P(None, "shot", "sub", None),
        P(None, "shot", "sub", None),
        P("shot", None, "sub", None, None),
        P("shot", "sub", None),
        P("shot"),
    )
    return jax.shard_map(
        functools.partial(on_device, mesh.shape["shot"], mesh.shape["sub"]),
        mesh=mesh,
        in_specs=placed,
        out_specs=P(None, "shot", "sub", None),
        check_vma=False,
    )
```
